32 devices in a mesh: layer: 4 (over y, x), tile: 8 (over z, core).
Axes of the slice: x: 2, y: 2, z: 4, core: 2. Of those that a mesh axis runs over, the one named last changes fastest.
Arguments:
- blocks: bfloat16 [2560, 9, 128, 128], P(('layer', 'tile')), may hold values from -6 to 6
- prolong: bfloat16 [2560, 2048], P(('layer', 'tile')), may hold values from -0.5 to 0.5
- columns: int32 [2560, 9], P(('layer', 'tile')), may hold values from -1 to 143, as said below
- aggregate: int32 [2560], P(('layer', 'tile')), may hold values from 0 to 59, as said below
- coarse_slot: int32 [2560, 9], P(('layer', 'tile')), may hold values from 0 to 31
- send_rows: int32 [256, 8], P(('layer', 'tile')), may hold values from 0 to 79
Outputs:
- coarse: float32 [640, 8192], P(('layer', 'tile'))
The draws below stay inside these ranges and needn't reach their ends.
Inputs may be any that keep to these rules, and one draw needn't show every extreme that they name: `columns`: slot 0 of every row is the row itself. A received code 80 + j * 8 + s appears in a device's rows if and only if the device has a neighbour in direction j (no wrap at the ends of the axes), and then every such code appears; -1 marks an absent block. `aggregate`: codes of a row i on its device are congruent to (i % 80) // 4 modulo 20. Codes of the second range never stand on the last tile, of the third never on the last layer.
All inputs are finite; a program needn't handle non-finite values.
Results may differ from the reference program's by a relative error of at most 0.0003.
Values may be sent and summed in bfloat16 or wider, within the bound.
A program may use at most 128 MiB of HBM per device.

```python
import jax
import jax.numpy as jnp
from jax import lax

FINE_DEV = 80
K = 9
BLK = 128
NN = 16
GA = 4
CS = 32
HCAP = 8
AGG_DEV = 20
LAYERS = 4
TILES = 8
NFINE = 2560


def draw_columns(key, part):
    key = jax.random.fold_in(key, 5)
    devices = LAYERS * TILES
    ghosts = 8 * HCAP
    extra = FINE_DEV * (K - 1)
    direction = jnp.arange(8, dtype=jnp.int32)
    offset = direction + (direction >= 4).astype(jnp.int32)
    layer_step = offset // 3 - 1
    tile_step = offset % 3 - 1

    def one_device(index):
        sub = jax.random.fold_in(key, index)
        layer_index = index // TILES
        tile_index = index % TILES
        peer_layer = layer_index + layer_step
        peer_tile = tile_index + tile_step
        valid = (peer_layer >= 0) & (peer_layer < LAYERS) & (peer_tile >= 0) & (peer_tile < TILES)
        order = jax.random.permutation(jax.random.fold_in(sub, 1), extra).astype(jnp.int32)
        pick = jax.random.randint(jax.random.fold_in(sub, 2), (extra,), 0, FINE_DEV + ghosts)
        rate = jax.random.randint(jax.random.fold_in(sub, 3), (), 10, 101)
        rate = jnp.where(index == 0, 50, rate)
        roll = jax.random.randint(jax.random.fold_in(sub, 4), (extra,), 0, 100)
        value = jnp.where(order < ghosts, FINE_DEV + order, jnp.where(roll < rate, pick, -1))
        which = jnp.clip((value - FINE_DEV) // HCAP, 0, 7)
        allowed = valid[which]
        value = jnp.where((value >= FINE_DEV) & jnp.logical_not(allowed), pick % FINE_DEV, value)
        value = value.reshape(FINE_DEV, K - 1).astype(jnp.int32)
        itself = jnp.arange(FINE_DEV, dtype=jnp.int32)[:, None]
        return jnp.concatenate([itself, value], axis=1)
    drawn = jax.vmap(one_device)(jnp.arange(devices, dtype=jnp.int32))
    return drawn.reshape(devices * FINE_DEV, K).astype(jnp.int32)


def draw_aggregate(key, part):
    key = jax.random.fold_in(key, 11)
    devices = LAYERS * TILES
    row = jnp.arange(devices * FINE_DEV, dtype=jnp.int32)
    device = row // FINE_DEV
    local = row % FINE_DEV
    layer = device // TILES
    tile = device % TILES
    group = local // GA
    roll = jax.random.randint(key, row.shape, 0, 8)
    kind = jnp.where(roll < 5, 0, jnp.where(roll < 7, 1, 2))
    kind = jnp.where(local == FINE_DEV - 1, 2, jnp.where(local == FINE_DEV - 2, 1, kind))
    kind = jnp.where(local == 0, 0, kind)
    kind = jnp.where((kind == 1) & (tile == TILES - 1), 0, kind)
    kind = jnp.where((kind == 2) & (layer == LAYERS - 1), 0, kind)
    return (kind * AGG_DEV + group).astype(jnp.int32)


def touch_ends(result, key, least, top_value):
    longest = result.shape.index(max(result.shape))
    spots = []
    for shift in (0, 1):
        where = [jax.random.randint(jax.random.fold_in(key, axis), (), 0, length) for axis, length in enumerate(result.shape)]
        where[longest] = (where[longest] + shift) % result.shape[longest]
        spots.append(tuple(where))
    return result.at[spots[0]].set(least).at[spots[1]].set(top_value)


def level_of(stream_key, dims, pieces, low, top_value):
    loudness, own = 1.0, jax.random.fold_in(stream_key, 6)
    for axis_at, parts in pieces:
        draws = jnp.exp(jax.random.uniform(jax.random.fold_in(own, axis_at), (parts,), jnp.float32, low / len(pieces), top_value / len(pieces)))
        loudness = loudness * jnp.repeat(draws, dims[axis_at] // parts).reshape([-1 if axis == axis_at else 1 for axis in range(len(dims))])
    return loudness


def gaussian(stream_key, dims, spread, limit, pieces=(), kind=jnp.bfloat16):
    values = spread * jax.random.normal(stream_key, dims, jnp.float32)
    if pieces:
        values = values * level_of(stream_key, dims, pieces, -0.22, 0.18)
    return jnp.clip(values, -limit, limit).astype(kind)


def setup_inputs(seed: int = 0) -> dict:
    seeds = jax.random.split(jax.random.key(seed), 7)
    return {
        "blocks": gaussian(seeds[0], (NFINE, K, BLK, BLK), 1.0, 6.0, ((0, 32),)),
        "prolong": gaussian(seeds[1], (NFINE, BLK * NN), BLK ** -0.5, 0.5, ((0, 32),)),
        "columns": draw_columns(jax.random.fold_in(seeds[6], 71), 0),
        "aggregate": draw_aggregate(jax.random.fold_in(seeds[6], 71), 0),
        "coarse_slot": touch_ends(jax.random.randint(seeds[4], (NFINE, K), 0, CS), jax.random.fold_in(seeds[4], 1), 0, CS - 1).astype(jnp.int32),
        "send_rows": touch_ends(jax.random.randint(seeds[5], (LAYERS * TILES * 8, HCAP), 0, FINE_DEV), jax.random.fold_in(seeds[5], 1), 0, FINE_DEV - 1).astype(jnp.int32),
    }


def reference(blocks, prolong, columns, aggregate, coarse_slot, send_rows):
    devices = LAYERS * TILES
    width = CS * NN * NN
    sends = send_rows.reshape(devices, 8, HCAP)
    basis = prolong.reshape(devices * FINE_DEV, BLK, NN)
    highest = lax.Precision.HIGHEST

    def one_device(device):
        start = (device * FINE_DEV).astype(jnp.int32)
        layer_index = device // TILES
        tile_index = device % TILES
        cols = lax.dynamic_slice_in_dim(columns, start, FINE_DEV, 0)
        ghost = jnp.maximum(cols - FINE_DEV, 0)
        direction = ghost // HCAP
        spot = ghost % HCAP
        offset = direction + (direction >= 4).astype(jnp.int32)
        layer_step = offset // 3 - 1
        tile_step = offset % 3 - 1
        peer_layer = jnp.clip(layer_index + layer_step, 0, LAYERS - 1)
        peer_tile = jnp.clip(tile_index + tile_step, 0, TILES - 1)
        peer = (peer_layer * TILES + peer_tile).astype(jnp.int32)
        remote = peer * FINE_DEV + sends[peer, 7 - direction, spot]
        located = jnp.where(cols < FINE_DEV, start + jnp.maximum(cols, 0), remote).astype(jnp.int32)
        fetched = basis[located].astype(jnp.float32)
        local_blocks = lax.dynamic_slice_in_dim(blocks, start, FINE_DEV, 0).astype(jnp.float32)
        product = jnp.einsum("rkab,rkbn->rkan", local_blocks, fetched, precision=highest)
        own_basis = lax.dynamic_slice_in_dim(basis, start, FINE_DEV, 0).astype(jnp.float32)
        terms = jnp.einsum("ram,rkan->rkmn", own_basis, product, precision=highest)
        terms = jnp.where((cols >= 0)[:, :, None, None], terms, jnp.float32(0.0))
        slots = lax.dynamic_slice_in_dim(coarse_slot, start, FINE_DEV, 0)
        slot_pick = (slots[:, :, None] == jnp.arange(CS, dtype=jnp.int32)[None, None, :]).astype(jnp.float32)
        row_terms = jnp.einsum("rks,rkmn->rsmn", slot_pick, terms, precision=highest).reshape(FINE_DEV, width)
        codes = lax.dynamic_slice_in_dim(aggregate, start, FINE_DEV, 0)
        picker = (codes[:, None] == jnp.arange(3 * AGG_DEV, dtype=jnp.int32)[None, :]).astype(jnp.float32)
        return jnp.dot(picker.T, row_terms, precision=highest, preferred_element_type=jnp.float32)

    partial_value = lax.map(one_device, jnp.arange(devices, dtype=jnp.int32))
    partial_value = partial_value.reshape(LAYERS, TILES, 3, AGG_DEV, width)
    coarse = partial_value[:, :, 0]
    coarse = coarse.at[:, 1:].add(partial_value[:, :-1, 1])
    coarse = coarse.at[1:].add(partial_value[:-1, :, 2])
    return coarse.reshape(devices * AGG_DEV, width)
```

```python
import jax
import jax.numpy as jnp
from jax import lax
from jax.experimental import pallas as pl
from jax.experimental.pallas import tpu as pltpu
from jax.sharding import PartitionSpec as P

CS = 32
LANES = 128
MESH = pl.DeviceIdType.MESH
F32 = jnp.float32
BF16 = jnp.bfloat16


def iota(shape, dim):
    return lax.broadcasted_iota(jnp.int32, shape, dim)


def ones_where(cond):
    return jnp.where(cond, jnp.float32(1.0), jnp.float32(0.0))


def directions():
    return [(q // 3 - 1, q % 3 - 1) for q in range(9) if q != 4]


def block_transpose(x):
    i = iota((8, LANES), 0)
    j = iota((8, LANES), 1) // 16
    for d in (1, 2, 4):
        up = pltpu.roll(pltpu.roll(x, d, 0), LANES - 16 * d, 1)
        down = up if d == 4 else pltpu.roll(pltpu.roll(x, 8 - d, 0), 16 * d, 1)
        bi = (i // d) % 2
        bj = (j // d) % 2
        x = jnp.where(bi == bj, x, jnp.where(bi > bj, up, down))
    return x


def make_kernel(layers, tiles, rows, links, hcap, ga):
    aggs = rows // ga
    ghosts = 8 * hcap

    def kernel(
        columns, aggregate, slots, sends, x_ref, blocks,
        out,
        bbuf, table, stage, ghost, qbuf, own, to_tile, to_layer, from_tile, from_layer, lane_mask, slot_mask,
        b_sem, gs_sem, gr_sem, ts_sem, tr_sem, ls_sem, lr_sem,
    ):
        layer = lax.axis_index("layer")
        tile = lax.axis_index("tile")

        def load_blocks(g):
            return pltpu.make_async_copy(
                blocks.at[pl.ds(g * ga, ga)], bbuf.at[pl.ds(g * ga, ga)], b_sem.at[g]
            )

        @pl.loop(0, aggs)
        def _(g):
            load_blocks(g).start()

        dirs = []
        for dl, dt in directions():
            pl_, pt_ = layer + dl, tile + dt
            ok = (pl_ >= 0) & (pl_ < layers) & (pt_ >= 0) & (pt_ < tiles)
            dirs.append((ok, pl_, pt_))

        barrier = pltpu.get_barrier_semaphore()
        for ok, a, b in dirs:
            @pl.when(ok)
            def _():
                pl.semaphore_signal(barrier, inc=1, device_id=(a, b), device_id_type=MESH)

        for j in range(8):
            for s in range(hcap):
                stage[j, s * 16:(s + 1) * 16, :] = x_ref[sends[j, s]]

        peers = sum(jnp.where(ok, 1, 0) for ok, _, _ in dirs)
        pl.semaphore_wait(barrier, peers)

        def ghost_copy(j):
            ok, a, b = dirs[j]
            return pltpu.make_async_remote_copy(
                src_ref=stage.at[j],
                dst_ref=ghost.at[7 - j],
                send_sem=gs_sem.at[j],
                recv_sem=gr_sem.at[7 - j],
                device_id=(a, b),
                device_id_type=MESH,
            )

        for j in range(8):
            @pl.when(dirs[j][0])
            def _():
                ghost_copy(j).start()

        spread = ones_where(iota((128, 16), 0) // 8 == iota((128, 16), 1)).astype(BF16)
        keep = ones_where(iota((128, LANES), 1) // 16 == iota((128, LANES), 0) % 8)
        fold = ones_where(iota((LANES, LANES), 0) % 16 == iota((LANES, LANES), 1) % 16).astype(BF16)
        pick = ones_where(iota((16, LANES), 1) % 16 == iota((16, LANES), 0)).astype(BF16)
        for v in range(9):
            lane_mask[v] = ones_where(iota((16, LANES), 1) // 16 == v - 1).astype(BF16)
        for v in range(4):
            slot_mask[v] = ones_where(iota((64, LANES), 0) // 16 == v).astype(BF16)

        def expand(x):
            y = jnp.dot(spread, x, preferred_element_type=F32)
            return (y * keep).astype(BF16)

        @pl.loop(0, aggs)
        def _(g):
            load_blocks(g).wait()
            for r in range(ga):
                i = g * ga + r
                y = expand(x_ref[i])
                table[i] = jnp.dot(y, fold, preferred_element_type=F32).astype(BF16)
                turned = lax.dot_general(
                    pick, y, (((1,), (1,)), ((), ())), preferred_element_type=F32
                ).astype(BF16)
                row = jnp.concatenate([bbuf[i, k] for k in range(links)], axis=1)
                q = jnp.dot(turned, row, preferred_element_type=F32)
                hi = q.astype(BF16)
                qbuf[i, :16, :] = hi
                qbuf[i, 16:, :] = (q - hi.astype(F32)).astype(BF16)

        for j in range(8):
            ok = dirs[j][0]

            @pl.when(ok)
            def _():
                ghost_copy(j).wait_send()

            @pl.when(dirs[7 - j][0])
            def _():
                ghost_copy(j).wait_recv()

            @pl.when(jnp.logical_not(dirs[7 - j][0]))
            def _():
                ghost[7 - j] = jnp.zeros((hcap * 16, LANES), BF16)

        for j in range(8):
            @pl.loop(0, hcap // 4)
            def _(h):
                for r in range(4):
                    s = h * 4 + r
                    y = expand(ghost[j, pl.ds(pl.multiple_of(s * 16, 16), 16), :])
                    table[rows + j * hcap + s] = jnp.dot(
                        y, fold, preferred_element_type=F32
                    ).astype(BF16)

        def tile_copy(g):
            return pltpu.make_async_remote_copy(
                src_ref=to_tile.at[g],
                dst_ref=from_tile.at[g],
                send_sem=ts_sem.at[g],
                recv_sem=tr_sem.at[g],
                device_id=(layer, tile + 1),
                device_id_type=MESH,
            )

        def layer_copy(g):
            return pltpu.make_async_remote_copy(
                src_ref=to_layer.at[g],
                dst_ref=from_layer.at[g],
                send_sem=ls_sem.at[g],
                recv_sem=lr_sem.at[g],
                device_id=(layer + 1, tile),
                device_id_type=MESH,
            )

        has_next_tile = tile < tiles - 1
        has_next_layer = layer < layers - 1
        has_prev_tile = tile > 0
        has_prev_layer = layer > 0

        @pl.loop(0, aggs)
        def _(g):
            sums = [jnp.zeros((64, LANES), F32) for _ in range(3)]
            for r in range(ga):
                i = g * ga + r
                right = []
                left = []
                for k in range(links):
                    c = columns[i, k]
                    s = slots[i, k]
                    v = jnp.where(c >= 0, s % 8 + 1, 0)
                    right.append(table[jnp.maximum(c, 0)] * jnp.concatenate([lane_mask[v]] * 8, axis=0))
                    m = slot_mask[s // 8]
                    hi = qbuf[i, :16, k * 128:(k + 1) * 128]
                    lo = qbuf[i, 16:, k * 128:(k + 1) * 128]
                    left.append(
                        jnp.concatenate(
                            [jnp.concatenate([hi] * 4, axis=0) * m, jnp.concatenate([lo] * 4, axis=0) * m], axis=0
                        )
                    )
                both = jnp.dot(
                    jnp.concatenate(left, axis=1),
                    jnp.concatenate(right, axis=0),
                    preferred_element_type=F32,
                )
                term = both[:64] + both[64:]
                a = aggregate[i]
                sums[0] += term * jnp.where(a < aggs, jnp.float32(1), jnp.float32(0))
                sums[1] += term * jnp.where((a >= aggs) & (a < 2 * aggs), jnp.float32(1), jnp.float32(0))
                sums[2] += term * jnp.where(a >= 2 * aggs, jnp.float32(1), jnp.float32(0))
            own[g] = sums[0]
            to_tile[g] = sums[1]
            to_layer[g] = sums[2]

            @pl.when(has_next_layer)
            def _():
                layer_copy(g).start()

            @pl.when(has_next_tile)
            def _():
                tile_copy(g).start()

        @pl.when(jnp.logical_not(has_prev_tile))
        def _():
            from_tile[...] = jnp.zeros_like(from_tile)

        @pl.when(jnp.logical_not(has_prev_layer))
        def _():
            from_layer[...] = jnp.zeros_like(from_layer)

        @pl.loop(0, aggs)
        def _(g):
            @pl.when(has_prev_tile)
            def _():
                tile_copy(g).wait_recv()

            @pl.when(has_prev_layer)
            def _():
                layer_copy(g).wait_recv()

            for q in range(4):
                for h in range(2):
                    at = slice(q * 16 + h * 8, q * 16 + h * 8 + 8)
                    total = own[g, at, :] + from_tile[g, at, :] + from_layer[g, at, :]
                    out[g, pl.ds(q * 16 + h, 8, stride=2), :] = block_transpose(total)

        @pl.loop(0, aggs)
        def _(g):
            @pl.when(has_next_tile)
            def _():
                tile_copy(g).wait_send()

            @pl.when(has_next_layer)
            def _():
                layer_copy(g).wait_send()

    return kernel


def solution(mesh):
    layers = mesh.shape["layer"]
    tiles = mesh.shape["tile"]

    def per_device(blocks, prolong, columns, aggregate, coarse_slot, send_rows):
        rows, links = columns.shape
        blk = blocks.shape[2]
        nnull = prolong.shape[1] // blk
        hcap = send_rows.shape[1]
        ga = 4
        aggs = rows // ga
        x = prolong.reshape(rows, nnull, blk)
        smem = pl.BlockSpec(memory_space=pltpu.SMEM)
        vmem = pl.BlockSpec(memory_space=pltpu.VMEM)
        dma = pltpu.SemaphoreType.DMA
        part = pltpu.VMEM((aggs, 64, LANES), F32)
        flat = pl.pallas_call(
            make_kernel(layers, tiles, rows, links, hcap, ga),
            out_shape=jax.ShapeDtypeStruct((aggs, 64, LANES), F32),
            in_specs=[smem, smem, smem, smem, vmem, pl.BlockSpec(memory_space=pl.ANY)],
            out_specs=vmem,
            scratch_shapes=[
                pltpu.VMEM((rows, links, blk, blk), BF16),
                pltpu.VMEM((rows + 8 * hcap, blk, LANES), BF16),
                pltpu.VMEM((8, hcap * 16, LANES), BF16),
                pltpu.VMEM((8, hcap * 16, LANES), BF16),
                pltpu.VMEM((rows, 32, links * blk), BF16),
                part, part, part, part, part,
                pltpu.VMEM((9, 16, LANES), BF16),
                pltpu.VMEM((4, 64, LANES), BF16),
                dma((aggs,)), dma((8,)), dma((8,)),
                dma((aggs,)), dma((aggs,)), dma((aggs,)), dma((aggs,)),
            ],
            compiler_params=pltpu.CompilerParams(
                collective_id=0, has_side_effects=True, vmem_limit_bytes=56 * 1024 * 1024
            ),
            cost_estimate=pl.CostEstimate(
                flops=2 * rows * links * blk * blk * nnull, bytes_accessed=rows * links * blk * blk * 2, transcendentals=0
            ),
        )(columns, aggregate, coarse_slot, send_rows, x, blocks)
        return flat.reshape(aggs, 64 * LANES)

    return jax.shard_map(
        per_device,
        mesh=mesh,
        in_specs=(
            P(("layer", "tile"), None, None, None),
            P(("layer", "tile"), None),
            P(("layer", "tile"), None),
            P(("layer", "tile")),
            P(("layer", "tile"), None),
            P(("layer", "tile"), None),
        ),
        out_specs=P(("layer", "tile"), None),
        check_vma=False,
    )
```

```python
import jax
import jax.numpy as jnp
from jax import lax
from jax.experimental import pallas as pl
from jax.experimental.pallas import tpu as pltpu
from jax.sharding import PartitionSpec as P

CS = 32
LANES = 128
MESH = pl.DeviceIdType.MESH
F32 = jnp.float32
BF16 = jnp.bfloat16


def iota(shape, dim):
    return lax.broadcasted_iota(jnp.int32, shape, dim)


def ones_where(cond):
    return jnp.where(cond, jnp.float32(1.0), jnp.float32(0.0))


def directions():
    return [(q // 3 - 1, q % 3 - 1) for q in range(9) if q != 4]


def block_transpose(x):
    i = iota((8, LANES), 0)
    j = iota((8, LANES), 1) // 16
    for d in (1, 2, 4):
        up = pltpu.roll(pltpu.roll(x, d, 0), LANES - 16 * d, 1)
        down = up if d == 4 else pltpu.roll(pltpu.roll(x, 8 - d, 0), 16 * d, 1)
        bi = (i // d) % 2
        bj = (j // d) % 2
        x = jnp.where(bi == bj, x, jnp.where(bi > bj, up, down))
    return x


def make_kernel(layers, tiles, rows, links, hcap, ga):
    aggs = rows // ga
    ghosts = 8 * hcap

    def kernel(
        columns, aggregate, slots, sends, x_ref, blocks,
        out,
        bbuf, table, stage, ghost, qbuf, own, to_tile, to_layer, from_tile, from_layer, lane_mask, slot_mask,
        spread, spread_ghost, turned, final,
        b_sem, gs_sem, gr_sem, ts_sem, tr_sem, ls_sem, lr_sem,
    ):
        layer = lax.axis_index("layer")
        tile = lax.axis_index("tile")

        def load_blocks(g):
            return pltpu.make_async_copy(
                blocks.at[pl.ds(g * ga, ga)], bbuf.at[pl.ds(g * ga, ga)], b_sem.at[g]
            )

        @pl.loop(0, aggs)
        def _(g):
            load_blocks(g).start()

        dirs = []
        for dl, dt in directions():
            pl_, pt_ = layer + dl, tile + dt
            ok = (pl_ >= 0) & (pl_ < layers) & (pt_ >= 0) & (pt_ < tiles)
            dirs.append((ok, pl_, pt_))

        barrier = pltpu.get_barrier_semaphore()
        for ok, a, b in dirs:
            @pl.when(ok)
            def _():
                pl.semaphore_signal(barrier, inc=1, device_id=(a, b), device_id_type=MESH)

        wanted = []
        for j in range(8):
            row = jnp.zeros((hcap, rows), jnp.int32)
            for s in range(hcap):
                row = jnp.where(iota((hcap, rows), 0) == s, sends[j, s], row)
            wanted.append(ones_where(row == iota((hcap, rows), 1)))
        gathered = jnp.dot(
            jnp.concatenate(wanted, axis=0).astype(BF16), x_ref[...], preferred_element_type=F32
        )
        for j in range(8):
            part = gathered[j * hcap:(j + 1) * hcap]
            stage[j] = jnp.concatenate(
                [part[:, m * LANES:(m + 1) * LANES] for m in range(16)], axis=0
            ).astype(BF16)

        peers = sum(jnp.where(ok, 1, 0) for ok, _, _ in dirs)
        pl.semaphore_wait(barrier, peers)

        def ghost_copy(j):
            ok, a, b = dirs[j]
            return pltpu.make_async_remote_copy(
                src_ref=stage.at[j],
                dst_ref=ghost.at[7 - j],
                send_sem=gs_sem.at[j],
                recv_sem=gr_sem.at[7 - j],
                device_id=(a, b),
                device_id_type=MESH,
            )

        for j in range(8):
            @pl.when(dirs[j][0])
            def _():
                ghost_copy(j).start()

        for h in range(16):
            spread[h * 128:(h + 1) * 128, :] = ones_where(
                iota((128, 256), 1) == iota((128, 256), 0) // 8 * 16 + h
            ).astype(BF16)
        for h in range(hcap):
            spread_ghost[h * 128:(h + 1) * 128, :] = ones_where(
                iota((128, 16 * hcap), 1) == iota((128, 16 * hcap), 0) // 8 * hcap + h
            ).astype(BF16)
        keep = ones_where(iota((128, LANES), 1) // 16 == iota((128, LANES), 0) % 8)
        fold = ones_where(iota((LANES, LANES), 0) % 16 == iota((LANES, LANES), 1) % 16).astype(BF16)
        pick = ones_where(iota((16, LANES), 1) % 16 == iota((16, LANES), 0)).astype(BF16)
        for v in range(9):
            lane_mask[v] = ones_where(iota((16, LANES), 1) // 16 == v - 1).astype(BF16)
        for v in range(4):
            slot_mask[v] = ones_where(iota((64, LANES), 0) // 16 == v).astype(BF16)

        def expand(picker, x, count, at):
            y = jnp.dot(picker, x, preferred_element_type=F32)
            y = jnp.concatenate(
                [(y[e * 128:(e + 1) * 128] * keep).astype(BF16) for e in range(count)], axis=0
            )
            t = jnp.dot(y, fold, preferred_element_type=F32).astype(BF16)
            for e in range(count):
                table[at + e] = t[e * 128:(e + 1) * 128]
            return y

        @pl.loop(0, rows // 16)
        def _(h):
            at = pl.multiple_of(h * 16, 16)
            for half in range(2):
                y = expand(
                    spread[half * 1024:(half + 1) * 1024, :],
                    jnp.concatenate(
                        [x_ref[pl.ds(at, 16), m * LANES:(m + 1) * LANES] for m in range(16)], axis=0
                    ),
                    8,
                    at + half * 8,
                )
                flipped = lax.dot_general(
                    pick, y, (((1,), (1,)), ((), ())), preferred_element_type=F32
                ).astype(BF16)
                for e in range(8):
                    turned[at + half * 8 + e] = flipped[:, e * 128:(e + 1) * 128]

        @pl.loop(0, aggs)
        def _(g):
            load_blocks(g).wait()
            for r in range(ga):
                i = g * ga + r
                row = jnp.concatenate([bbuf[i, k] for k in range(links)], axis=1)
                q = jnp.dot(turned[i], row, preferred_element_type=F32)
                hi = q.astype(BF16)
                qbuf[i, :16, :] = hi
                qbuf[i, 16:, :] = (q - hi.astype(F32)).astype(BF16)

        for j in range(8):
            ok = dirs[j][0]

            @pl.when(ok)
            def _():
                ghost_copy(j).wait_send()

            @pl.when(dirs[7 - j][0])
            def _():
                ghost_copy(j).wait_recv()

            @pl.when(jnp.logical_not(dirs[7 - j][0]))
            def _():
                ghost[7 - j] = jnp.zeros((hcap * 16, LANES), BF16)

        @pl.loop(0, 8)
        def _(j):
            expand(spread_ghost[...], ghost[j], hcap, rows + j * hcap)

        def tile_copy(g):
            return pltpu.make_async_remote_copy(
                src_ref=to_tile.at[g],
                dst_ref=from_tile.at[g],
                send_sem=ts_sem.at[g],
                recv_sem=tr_sem.at[g],
                device_id=(layer, tile + 1),
                device_id_type=MESH,
            )

        def layer_copy(g):
            return pltpu.make_async_remote_copy(
                src_ref=to_layer.at[g],
                dst_ref=from_layer.at[g],
                send_sem=ls_sem.at[g],
                recv_sem=lr_sem.at[g],
                device_id=(layer + 1, tile),
                device_id_type=MESH,
            )

        has_next_tile = tile < tiles - 1
        has_next_layer = layer < layers - 1
        has_prev_tile = tile > 0
        has_prev_layer = layer > 0

        @pl.loop(0, aggs)
        def _(g):
            sums = [jnp.zeros((64, LANES), F32) for _ in range(3)]
            for r in range(ga):
                i = g * ga + r
                right = []
                left = []
                for k in range(links):
                    c = columns[k, i]
                    s = slots[k, i]
                    v = jnp.where(c >= 0, s % 8 + 1, 0)
                    right.append(table[jnp.maximum(c, 0)] * jnp.concatenate([lane_mask[v]] * 8, axis=0))
                    m = slot_mask[s // 8]
                    hi = qbuf[i, :16, k * 128:(k + 1) * 128]
                    lo = qbuf[i, 16:, k * 128:(k + 1) * 128]
                    left.append(
                        jnp.concatenate(
                            [jnp.concatenate([hi] * 4, axis=0) * m, jnp.concatenate([lo] * 4, axis=0) * m], axis=0
                        )
                    )
                both = jnp.dot(
                    jnp.concatenate(left, axis=1),
                    jnp.concatenate(right, axis=0),
                    preferred_element_type=F32,
                )
                term = both[:64] + both[64:]
                a = aggregate[i]
                sums[0] += term * jnp.where(a < aggs, jnp.float32(1), jnp.float32(0))
                sums[1] += term * jnp.where((a >= aggs) & (a < 2 * aggs), jnp.float32(1), jnp.float32(0))
                sums[2] += term * jnp.where(a >= 2 * aggs, jnp.float32(1), jnp.float32(0))
            own[g] = sums[0]
            to_tile[g] = sums[1]
            to_layer[g] = sums[2]

            @pl.when(has_next_layer)
            def _():
                layer_copy(g).start()

            @pl.when(has_next_tile)
            def _():
                tile_copy(g).start()

        @pl.when(jnp.logical_not(has_prev_tile))
        def _():
            from_tile[...] = jnp.zeros_like(from_tile)

        @pl.when(jnp.logical_not(has_prev_layer))
        def _():
            from_layer[...] = jnp.zeros_like(from_layer)

        @pl.loop(0, aggs)
        def _(g):
            @pl.when(has_prev_tile)
            def _():
                tile_copy(g).wait_recv()

            @pl.when(has_prev_layer)
            def _():
                layer_copy(g).wait_recv()

            for q in range(4):
                for h in range(2):
                    at = slice(q * 16 + h * 8, q * 16 + h * 8 + 8)
                    total = own[g, at, :] + from_tile[g, at, :] + from_layer[g, at, :]
                    final[pl.ds((q * 16 + h) * 24 + g, 8, stride=48), :] = block_transpose(total)

        @pl.loop(0, aggs)
        def _(g):
            @pl.when(has_next_tile)
            def _():
                tile_copy(g).wait_send()

            @pl.when(has_next_layer)
            def _():
                layer_copy(g).wait_send()

        for m in range(64):
            out[:, m * LANES:(m + 1) * LANES] = final[m * 24:m * 24 + aggs, :]

    return kernel


def solution(mesh):
    layers = mesh.shape["layer"]
    tiles = mesh.shape["tile"]

    def per_device(blocks, prolong, columns, aggregate, coarse_slot, send_rows):
        rows, links = columns.shape
        blk = blocks.shape[2]
        nnull = prolong.shape[1] // blk
        hcap = send_rows.shape[1]
        ga = 4
        aggs = rows // ga
        smem = pl.BlockSpec(memory_space=pltpu.SMEM)
        vmem = pl.BlockSpec(memory_space=pltpu.VMEM)
        dma = pltpu.SemaphoreType.DMA
        part = pltpu.VMEM((aggs, 64, LANES), F32)
        return pl.pallas_call(
            make_kernel(layers, tiles, rows, links, hcap, ga),
            out_shape=jax.ShapeDtypeStruct((aggs, 64 * LANES), F32),
            in_specs=[smem, smem, smem, smem, vmem, pl.BlockSpec(memory_space=pl.ANY)],
            out_specs=vmem,
            scratch_shapes=[
                pltpu.VMEM((rows, links, blk, blk), BF16),
                pltpu.VMEM((rows + 8 * hcap, blk, LANES), BF16),
                pltpu.VMEM((8, hcap * 16, LANES), BF16),
                pltpu.VMEM((8, hcap * 16, LANES), BF16),
                pltpu.VMEM((rows, 32, links * blk), BF16),
                part, part, part, part, part,
                pltpu.VMEM((9, 16, LANES), BF16),
                pltpu.VMEM((4, 64, LANES), BF16),
                pltpu.VMEM((2048, 256), BF16),
                pltpu.VMEM((128 * hcap, 16 * hcap), BF16),
                pltpu.VMEM((rows, 16, LANES), BF16),
                pltpu.VMEM((64 * 24, LANES), F32),
                dma((aggs,)), dma((8,)), dma((8,)),
                dma((aggs,)), dma((aggs,)), dma((aggs,)), dma((aggs,)),
            ],
            compiler_params=pltpu.CompilerParams(
                collective_id=0, has_side_effects=True, vmem_limit_bytes=56 * 1024 * 1024
            ),
            cost_estimate=pl.CostEstimate(
                flops=2 * rows * links * blk * blk * nnull, bytes_accessed=rows * links * blk * blk * 2, transcendentals=0
            ),
        )(columns.T, aggregate, coarse_slot.T, send_rows, prolong, blocks)

    return jax.shard_map(
        per_device,
        mesh=mesh,
        in_specs=(
            P(("layer", "tile"), None, None, None),
            P(("layer", "tile"), None),
            P(("layer", "tile"), None),
            P(("layer", "tile")),
            P(("layer", "tile"), None),
            P(("layer", "tile"), None),
        ),
        out_specs=P(("layer", "tile"), None),
        check_vma=False,
    )
```

```python
import jax
import jax.numpy as jnp
from jax import lax
from jax.experimental import pallas as pl
from jax.experimental.pallas import tpu as pltpu
from jax.sharding import PartitionSpec as P

LAG = 8
PITCH = 129
LANES = 128
MESH = pl.DeviceIdType.MESH
F32 = jnp.float32
BF16 = jnp.bfloat16


def iota(shape, dim):
    return lax.broadcasted_iota(jnp.int32, shape, dim)


def ones_where(cond):
    return jnp.where(cond, jnp.float32(1.0), jnp.float32(0.0))


def directions():
    return [(q // 3 - 1, q % 3 - 1) for q in range(9) if q != 4]


def block_transpose(x):
    i = iota((8, LANES), 0)
    j = iota((8, LANES), 1) // 16
    for d in (1, 2, 4):
        up = pltpu.roll(pltpu.roll(x, d, 0), LANES - 16 * d, 1)
        down = up if d == 4 else pltpu.roll(pltpu.roll(x, 8 - d, 0), 16 * d, 1)
        bi = (i // d) % 2
        bj = (j // d) % 2
        x = jnp.where(bi == bj, x, jnp.where(bi > bj, up, down))
    return x


def make_kernel(layers, tiles, rows, links, hcap, ga):
    aggs = rows // ga
    ghosts = 8 * hcap

    def kernel(
        columns, aggregate, slots, sends, x_ref, blocks,
        out,
        bbuf, table, stage, ghost, qbuf, own, to_tile, to_layer, from_tile, from_layer, lane_mask, slot_mask,
        wide, turned, final,
        b_sem, gs_sem, gr_sem, ts_sem, tr_sem, ls_sem, lr_sem,
    ):
        layer = lax.axis_index("layer")
        tile = lax.axis_index("tile")

        def load_blocks(g):
            return pltpu.make_async_copy(
                blocks.at[pl.ds(g * ga, ga)], bbuf.at[pl.ds(g * ga, ga)], b_sem.at[g]
            )

        @pl.loop(0, aggs)
        def _(g):
            load_blocks(g).start()

        dirs = []
        for dl, dt in directions():
            pl_, pt_ = layer + dl, tile + dt
            ok = (pl_ >= 0) & (pl_ < layers) & (pt_ >= 0) & (pt_ < tiles)
            dirs.append((ok, pl_, pt_))

        barrier = pltpu.get_barrier_semaphore()
        for ok, a, b in dirs:
            @pl.when(ok)
            def _():
                pl.semaphore_signal(barrier, inc=1, device_id=(a, b), device_id_type=MESH)

        wanted = []
        for j in range(8):
            row = jnp.zeros((hcap, rows), jnp.int32)
            for s in range(hcap):
                row = jnp.where(iota((hcap, rows), 0) == s, sends[j, s], row)
            wanted.append(ones_where(row == iota((hcap, rows), 1)))
        gathered = jnp.dot(
            jnp.concatenate(wanted, axis=0).astype(BF16), x_ref[...], preferred_element_type=F32
        )
        for j in range(8):
            part = gathered[j * hcap:(j + 1) * hcap]
            stage[j] = jnp.concatenate(
                [part[:, m * LANES:(m + 1) * LANES] for m in range(16)], axis=0
            ).astype(BF16)

        peers = sum(jnp.where(ok, 1, 0) for ok, _, _ in dirs)
        pl.semaphore_wait(barrier, peers)

        def ghost_copy(j):
            ok, a, b = dirs[j]
            return pltpu.make_async_remote_copy(
                src_ref=stage.at[j],
                dst_ref=ghost.at[7 - j],
                send_sem=gs_sem.at[j],
                recv_sem=gr_sem.at[7 - j],
                device_id=(a, b),
                device_id_type=MESH,
            )

        for j in range(8):
            @pl.when(dirs[j][0])
            def _():
                ghost_copy(j).start()

        place = jnp.concatenate(
            [
                ones_where(iota((LANES, LANES), 0) == iota((LANES, LANES), 1) % 16 + 16 * e).astype(BF16)
                for e in range(8)
            ],
            axis=1,
        )
        pick = ones_where(iota((16, LANES), 1) == iota((16, LANES), 0)).astype(BF16)
        for v in range(9):
            lane_mask[v] = ones_where(iota((16, LANES), 1) // 16 == v - 1).astype(BF16)
        for v in range(4):
            slot_mask[v] = ones_where(iota((64, LANES), 0) // 16 == v).astype(BF16)

        def expand(x, count, at):
            for h in range(4):
                y = jnp.dot(x, place[:, h * 256:(h + 1) * 256], preferred_element_type=F32)
                for m in range(16):
                    for c in range(0, count, 8):
                        for e in range(2):
                            wide[pl.ds(c * PITCH + 8 * m + 2 * h + e, 8, stride=PITCH), :] = y[
                                m * count + c:m * count + c + 8, e * 128:(e + 1) * 128
                            ]
            for c in range(count):
                table[at + c] = wide[c * PITCH:c * PITCH + 128, :].astype(BF16)

        @pl.loop(0, rows // 16)
        def _(h):
            at = pl.multiple_of(h * 16, 16)
            expand(
                jnp.concatenate(
                    [x_ref[pl.ds(at, 16), m * LANES:(m + 1) * LANES] for m in range(16)], axis=0
                ),
                16,
                at,
            )
            for half in range(2):
                y = jnp.concatenate([table[at + half * 8 + e] for e in range(8)], axis=0)
                flipped = lax.dot_general(
                    pick, y, (((1,), (1,)), ((), ())), preferred_element_type=F32
                ).astype(BF16)
                for e in range(8):
                    turned[at + half * 8 + e] = flipped[:, e * 128:(e + 1) * 128]

        @pl.loop(0, aggs)
        def _(g):
            load_blocks(g).wait()
            for r in range(ga):
                i = g * ga + r
                row = jnp.concatenate([bbuf[i, k] for k in range(links)], axis=1)
                q = jnp.dot(turned[i], row, preferred_element_type=F32)
                hi = q.astype(BF16)
                qbuf[i, :16, :] = hi
                qbuf[i, 16:, :] = (q - hi.astype(F32)).astype(BF16)

        for j in range(8):
            ok = dirs[j][0]

            @pl.when(ok)
            def _():
                ghost_copy(j).wait_send()

            @pl.when(dirs[7 - j][0])
            def _():
                ghost_copy(j).wait_recv()

            @pl.when(jnp.logical_not(dirs[7 - j][0]))
            def _():
                ghost[7 - j] = jnp.zeros((hcap * 16, LANES), BF16)

        @pl.loop(0, 8)
        def _(j):
            expand(ghost[j], hcap, rows + j * hcap)

        def tile_copy(g):
            return pltpu.make_async_remote_copy(
                src_ref=to_tile.at[g],
                dst_ref=from_tile.at[g],
                send_sem=ts_sem.at[g],
                recv_sem=tr_sem.at[g],
                device_id=(layer, tile + 1),
                device_id_type=MESH,
            )

        def layer_copy(g):
            return pltpu.make_async_remote_copy(
                src_ref=to_layer.at[g],
                dst_ref=from_layer.at[g],
                send_sem=ls_sem.at[g],
                recv_sem=lr_sem.at[g],
                device_id=(layer + 1, tile),
                device_id_type=MESH,
            )

        has_next_tile = tile < tiles - 1
        has_next_layer = layer < layers - 1
        has_prev_tile = tile > 0
        has_prev_layer = layer > 0

        @pl.when(jnp.logical_not(has_prev_tile))
        def _():
            from_tile[...] = jnp.zeros_like(from_tile)

        @pl.when(jnp.logical_not(has_prev_layer))
        def _():
            from_layer[...] = jnp.zeros_like(from_layer)

        def combine(g):
            sums = [jnp.zeros((64, LANES), F32) for _ in range(3)]
            for r in range(ga):
                i = g * ga + r
                right = []
                left = []
                for k in range(links):
                    c = columns[k, i]
                    s = slots[k, i]
                    v = jnp.where(c >= 0, (s & 7) + 1, 0)
                    right.append(table[jnp.maximum(c, 0)] * jnp.concatenate([lane_mask[v]] * 8, axis=0))
                    m = slot_mask[s >> 3]
                    hi = qbuf[i, :16, k * 128:(k + 1) * 128]
                    lo = qbuf[i, 16:, k * 128:(k + 1) * 128]
                    left.append(
                        jnp.concatenate(
                            [jnp.concatenate([hi] * 4, axis=0) * m, jnp.concatenate([lo] * 4, axis=0) * m], axis=0
                        )
                    )
                both = jnp.dot(
                    jnp.concatenate(left, axis=1),
                    jnp.concatenate(right, axis=0),
                    preferred_element_type=F32,
                )
                term = both[:64] + both[64:]
                a = aggregate[i]
                sums[0] += term * jnp.where(a < aggs, jnp.float32(1), jnp.float32(0))
                sums[1] += term * jnp.where((a >= aggs) & (a < 2 * aggs), jnp.float32(1), jnp.float32(0))
                sums[2] += term * jnp.where(a >= 2 * aggs, jnp.float32(1), jnp.float32(0))
            own[g] = sums[0]
            to_tile[g] = sums[1]
            to_layer[g] = sums[2]

        def send(g):
            @pl.when(has_next_layer)
            def _():
                layer_copy(g).start()

            @pl.when(has_next_tile)
            def _():
                tile_copy(g).start()

        def receive(g):
            @pl.when(has_prev_tile)
            def _():
                tile_copy(g).wait_recv()

            @pl.when(has_prev_layer)
            def _():
                layer_copy(g).wait_recv()

        def finish(g):
            for q in range(4):
                for h in range(2):
                    at = slice(q * 16 + h * 8, q * 16 + h * 8 + 8)
                    total = own[g, at, :] + from_tile[g, at, :] + from_layer[g, at, :]
                    final[pl.ds((q * 16 + h) * 24 + g, 8, stride=48), :] = block_transpose(total)

        @pl.loop(0, LAG)
        def _(g):
            combine(g)
            send(g)

        @pl.loop(LAG, aggs)
        def _(g):
            receive(g - LAG)
            finish(g - LAG)
            combine(g)
            send(g)

        @pl.loop(aggs - LAG, aggs)
        def _(g):
            receive(g)
            finish(g)

        @pl.loop(0, aggs)
        def _(g):
            @pl.when(has_next_tile)
            def _():
                tile_copy(g).wait_send()

            @pl.when(has_next_layer)
            def _():
                layer_copy(g).wait_send()

        for m in range(64):
            out[:, m * LANES:(m + 1) * LANES] = final[m * 24:m * 24 + aggs, :]

    return kernel


def solution(mesh):
    layers = mesh.shape["layer"]
    tiles = mesh.shape["tile"]

    def per_device(blocks, prolong, columns, aggregate, coarse_slot, send_rows):
        rows, links = columns.shape
        blk = blocks.shape[2]
        nnull = prolong.shape[1] // blk
        hcap = send_rows.shape[1]
        ga = 4
        aggs = rows // ga
        smem = pl.BlockSpec(memory_space=pltpu.SMEM)
        vmem = pl.BlockSpec(memory_space=pltpu.VMEM)
        dma = pltpu.SemaphoreType.DMA
        part = pltpu.VMEM((aggs, 64, LANES), F32)
        return pl.pallas_call(
            make_kernel(layers, tiles, rows, links, hcap, ga),
            out_shape=jax.ShapeDtypeStruct((aggs, 64 * LANES), F32),
            in_specs=[smem, smem, smem, smem, vmem, pl.BlockSpec(memory_space=pl.ANY)],
            out_specs=vmem,
            scratch_shapes=[
                pltpu.VMEM((rows, links, blk, blk), BF16),
                pltpu.VMEM((rows + 8 * hcap, blk, LANES), BF16),
                pltpu.VMEM((8, hcap * 16, LANES), BF16),
                pltpu.VMEM((8, hcap * 16, LANES), BF16),
                pltpu.VMEM((rows, 32, links * blk), BF16),
                part, part, part, part, part,
                pltpu.VMEM((9, 16, LANES), BF16),
                pltpu.VMEM((4, 64, LANES), BF16),
                pltpu.VMEM((16 * PITCH, LANES), F32),
                pltpu.VMEM((rows, 16, LANES), BF16),
                pltpu.VMEM((64 * 24, LANES), F32),
                dma((aggs,)), dma((8,)), dma((8,)),
                dma((aggs,)), dma((aggs,)), dma((aggs,)), dma((aggs,)),
            ],
            compiler_params=pltpu.CompilerParams(
                collective_id=0, has_side_effects=True, vmem_limit_bytes=56 * 1024 * 1024
            ),
            cost_estimate=pl.CostEstimate(
                flops=2 * rows * links * blk * blk * nnull, bytes_accessed=rows * links * blk * blk * 2, transcendentals=0
            ),
        )(columns.T, aggregate, coarse_slot.T, send_rows, prolong, blocks)

    return jax.shard_map(
        per_device,
        mesh=mesh,
        in_specs=(
            P(("layer", "tile"), None, None, None),
            P(("layer", "tile"), None),
            P(("layer", "tile"), None),
            P(("layer", "tile")),
            P(("layer", "tile"), None),
            P(("layer", "tile"), None),
        ),
        out_specs=P(("layer", "tile"), None),
        check_vma=False,
    )
```

```python
import jax
import jax.numpy as jnp
from jax import lax
from jax.experimental import pallas as pl
from jax.experimental.pallas import tpu as pltpu
from jax.sharding import PartitionSpec as P

LAG = 8
PITCH = 129
LANES = 128
MESH = pl.DeviceIdType.MESH
F32 = jnp.float32
BF16 = jnp.bfloat16


def iota(shape, dim):
    return lax.broadcasted_iota(jnp.int32, shape, dim)


def ones_where(cond):
    return jnp.where(cond, jnp.float32(1.0), jnp.float32(0.0))


def directions():
    return [(q // 3 - 1, q % 3 - 1) for q in range(9) if q != 4]


def block_transpose(x):
    i = iota((8, LANES), 0)
    j = iota((8, LANES), 1) // 16
    for d in (1, 2, 4):
        up = pltpu.roll(pltpu.roll(x, d, 0), LANES - 16 * d, 1)
        down = up if d == 4 else pltpu.roll(pltpu.roll(x, 8 - d, 0), 16 * d, 1)
        bi = (i // d) % 2
        bj = (j // d) % 2
        x = jnp.where(bi == bj, x, jnp.where(bi > bj, up, down))
    return x


def make_kernel(layers, tiles, rows, links, hcap, ga):
    aggs = rows // ga
    ghosts = 8 * hcap

    def kernel(
        columns, aggregate, slots, sends, x_ref, blocks,
        out,
        bbuf, table, stage, ghost, qbuf, own, to_tile, to_layer, from_tile, from_layer, lane_mask, slot_mask,
        wide, turned, final,
        b_sem, gs_sem, gr_sem, ts_sem, tr_sem, ls_sem, lr_sem,
    ):
        layer = lax.axis_index("layer")
        tile = lax.axis_index("tile")

        def load_blocks(g):
            return pltpu.make_async_copy(
                blocks.at[pl.ds(g * ga, ga)], bbuf.at[pl.ds(g * ga, ga)], b_sem.at[g]
            )

        @pl.loop(0, aggs)
        def _(g):
            load_blocks(g).start()

        dirs = []
        for dl, dt in directions():
            pl_, pt_ = layer + dl, tile + dt
            ok = (pl_ >= 0) & (pl_ < layers) & (pt_ >= 0) & (pt_ < tiles)
            dirs.append((ok, pl_, pt_))

        barrier = pltpu.get_barrier_semaphore()
        for ok, a, b in dirs:
            @pl.when(ok)
            def _():
                pl.semaphore_signal(barrier, inc=1, device_id=(a, b), device_id_type=MESH)

        wanted = []
        for j in range(8):
            row = jnp.zeros((hcap, rows), jnp.int32)
            for s in range(hcap):
                row = jnp.where(iota((hcap, rows), 0) == s, sends[j, s], row)
            wanted.append(ones_where(row == iota((hcap, rows), 1)))
        gathered = jnp.dot(
            jnp.concatenate(wanted, axis=0).astype(BF16), x_ref[...], preferred_element_type=F32
        )
        for j in range(8):
            part = gathered[j * hcap:(j + 1) * hcap]
            stage[j] = jnp.concatenate(
                [part[:, m * LANES:(m + 1) * LANES] for m in range(16)], axis=0
            ).astype(BF16)

        peers = sum(jnp.where(ok, 1, 0) for ok, _, _ in dirs)
        pl.semaphore_wait(barrier, peers)

        def ghost_copy(j):
            ok, a, b = dirs[j]
            return pltpu.make_async_remote_copy(
                src_ref=stage.at[j],
                dst_ref=ghost.at[7 - j],
                send_sem=gs_sem.at[j],
                recv_sem=gr_sem.at[7 - j],
                device_id=(a, b),
                device_id_type=MESH,
            )

        for j in range(8):
            @pl.when(dirs[j][0])
            def _():
                ghost_copy(j).start()

        place = jnp.concatenate(
            [
                ones_where(iota((LANES, LANES), 0) == iota((LANES, LANES), 1) % 16 + 16 * e).astype(BF16)
                for e in range(8)
            ],
            axis=1,
        )
        pick = ones_where(iota((16, LANES), 1) == iota((16, LANES), 0)).astype(BF16)
        for v in range(9):
            lane_mask[v] = ones_where(iota((16, LANES), 1) // 16 == v - 1).astype(BF16)
        for v in range(4):
            slot_mask[v] = ones_where(iota((64, LANES), 0) // 16 == v).astype(BF16)

        def expand(x, count, at, base=0):
            for h in range(4):
                y = jnp.dot(x, place[:, h * 256:(h + 1) * 256], preferred_element_type=F32)
                for m in range(16):
                    for c in range(0, count, 8):
                        for e in range(2):
                            wide[pl.ds(base + c * PITCH + 8 * m + 2 * h + e, 8, stride=PITCH), :] = y[
                                m * count + c:m * count + c + 8, e * 128:(e + 1) * 128
                            ]
            for c in range(count):
                table[at + c] = wide[base + c * PITCH:base + c * PITCH + 128, :].astype(BF16)

        @pl.loop(0, rows // 16)
        def _(h):
            at = pl.multiple_of(h * 16, 16)
            expand(
                jnp.concatenate(
                    [x_ref[pl.ds(at, 16), m * LANES:(m + 1) * LANES] for m in range(16)], axis=0
                ),
                16,
                at,
            )
            for half in range(2):
                y = jnp.concatenate([table[at + half * 8 + e] for e in range(8)], axis=0)
                flipped = lax.dot_general(
                    pick, y, (((1,), (1,)), ((), ())), preferred_element_type=F32
                ).astype(BF16)
                for e in range(8):
                    turned[at + half * 8 + e] = flipped[:, e * 128:(e + 1) * 128]

        @pl.loop(0, aggs)
        def _(g):
            load_blocks(g).wait()
            for r in range(ga):
                i = g * ga + r
                row = jnp.concatenate([bbuf[i, k] for k in range(links)], axis=1)
                q = jnp.dot(turned[i], row, preferred_element_type=F32)
                hi = q.astype(BF16)
                qbuf[i, :16, :] = hi
                qbuf[i, 16:, :] = (q - hi.astype(F32)).astype(BF16)

        for j in range(8):
            ok = dirs[j][0]

            @pl.when(ok)
            def _():
                ghost_copy(j).wait_send()

            @pl.when(dirs[7 - j][0])
            def _():
                ghost_copy(j).wait_recv()

            @pl.when(jnp.logical_not(dirs[7 - j][0]))
            def _():
                ghost[7 - j] = jnp.zeros((hcap * 16, LANES), BF16)

        @pl.loop(0, 4)
        def _(j):
            for e in range(2):
                expand(ghost[2 * j + e], hcap, rows + (2 * j + e) * hcap, e * 8 * PITCH)

        def tile_copy(g):
            return pltpu.make_async_remote_copy(
                src_ref=to_tile.at[g],
                dst_ref=from_tile.at[g],
                send_sem=ts_sem.at[g],
                recv_sem=tr_sem.at[g],
                device_id=(layer, tile + 1),
                device_id_type=MESH,
            )

        def layer_copy(g):
            return pltpu.make_async_remote_copy(
                src_ref=to_layer.at[g],
                dst_ref=from_layer.at[g],
                send_sem=ls_sem.at[g],
                recv_sem=lr_sem.at[g],
                device_id=(layer + 1, tile),
                device_id_type=MESH,
            )

        has_next_tile = tile < tiles - 1
        has_next_layer = layer < layers - 1
        has_prev_tile = tile > 0
        has_prev_layer = layer > 0

        @pl.when(jnp.logical_not(has_prev_tile))
        def _():
            from_tile[...] = jnp.zeros_like(from_tile)

        @pl.when(jnp.logical_not(has_prev_layer))
        def _():
            from_layer[...] = jnp.zeros_like(from_layer)

        def combine(g):
            sums = [jnp.zeros((64, LANES), F32) for _ in range(3)]
            for r in range(ga):
                i = g * ga + r
                right = []
                left = []
                for k in range(links):
                    c = columns[k, i]
                    s = slots[k, i]
                    v = jnp.where(c >= 0, (s & 7) + 1, 0)
                    right.append(table[jnp.maximum(c, 0)] * jnp.concatenate([lane_mask[v]] * 8, axis=0))
                    m = slot_mask[s >> 3]
                    hi = qbuf[i, :16, k * 128:(k + 1) * 128]
                    lo = qbuf[i, 16:, k * 128:(k + 1) * 128]
                    left.append(
                        jnp.concatenate(
                            [jnp.concatenate([hi] * 4, axis=0) * m, jnp.concatenate([lo] * 4, axis=0) * m], axis=0
                        )
                    )
                both = jnp.dot(
                    jnp.concatenate(left, axis=1),
                    jnp.concatenate(right, axis=0),
                    preferred_element_type=F32,
                )
                term = both[:64] + both[64:]
                a = aggregate[i]
                sums[0] += term * jnp.where(a < aggs, jnp.float32(1), jnp.float32(0))
                sums[1] += term * jnp.where((a >= aggs) & (a < 2 * aggs), jnp.float32(1), jnp.float32(0))
                sums[2] += term * jnp.where(a >= 2 * aggs, jnp.float32(1), jnp.float32(0))
            own[g] = sums[0]
            to_tile[g] = sums[1]
            to_layer[g] = sums[2]

        def send(g):
            @pl.when(has_next_layer)
            def _():
                layer_copy(g).start()

            @pl.when(has_next_tile)
            def _():
                tile_copy(g).start()

        def receive(g):
            @pl.when(has_prev_tile)
            def _():
                tile_copy(g).wait_recv()

            @pl.when(has_prev_layer)
            def _():
                layer_copy(g).wait_recv()

        def finish(g):
            for q in range(4):
                for h in range(2):
                    at = slice(q * 16 + h * 8, q * 16 + h * 8 + 8)
                    total = own[g, at, :] + from_tile[g, at, :] + from_layer[g, at, :]
                    final[pl.ds((q * 16 + h) * 25 + g, 8, stride=50), :] = block_transpose(total)

        @pl.loop(0, LAG)
        def _(g):
            combine(g)
            send(g)

        @pl.loop(LAG, aggs)
        def _(g):
            receive(g - LAG)
            finish(g - LAG)
            combine(g)
            send(g)

        @pl.loop(aggs - LAG, aggs)
        def _(g):
            receive(g)
            finish(g)

        @pl.loop(0, aggs)
        def _(g):
            @pl.when(has_next_tile)
            def _():
                tile_copy(g).wait_send()

            @pl.when(has_next_layer)
            def _():
                layer_copy(g).wait_send()

        for m in range(64):
            out[:, m * LANES:(m + 1) * LANES] = final[m * 25:m * 25 + aggs, :]

    return kernel


def solution(mesh):
    layers = mesh.shape["layer"]
    tiles = mesh.shape["tile"]

    def per_device(blocks, prolong, columns, aggregate, coarse_slot, send_rows):
        rows, links = columns.shape
        blk = blocks.shape[2]
        nnull = prolong.shape[1] // blk
        hcap = send_rows.shape[1]
        ga = 4
        aggs = rows // ga
        smem = pl.BlockSpec(memory_space=pltpu.SMEM)
        vmem = pl.BlockSpec(memory_space=pltpu.VMEM)
        dma = pltpu.SemaphoreType.DMA
        part = pltpu.VMEM((aggs, 64, LANES), F32)
        return pl.pallas_call(
            make_kernel(layers, tiles, rows, links, hcap, ga),
            out_shape=jax.ShapeDtypeStruct((aggs, 64 * LANES), F32),
            in_specs=[smem, smem, smem, smem, vmem, pl.BlockSpec(memory_space=pl.ANY)],
            out_specs=vmem,
            scratch_shapes=[
                pltpu.VMEM((rows, links, blk, blk), BF16),
                pltpu.VMEM((rows + 8 * hcap, blk, LANES), BF16),
                pltpu.VMEM((8, hcap * 16, LANES), BF16),
                pltpu.VMEM((8, hcap * 16, LANES), BF16),
                pltpu.VMEM((rows, 32, links * blk), BF16),
                part, part, part, part, part,
                pltpu.VMEM((9, 16, LANES), BF16),
                pltpu.VMEM((4, 64, LANES), BF16),
                pltpu.VMEM((16 * PITCH, LANES), F32),
                pltpu.VMEM((rows, 16, LANES), BF16),
                pltpu.VMEM((64 * 25, LANES), F32),
                dma((aggs,)), dma((8,)), dma((8,)),
                dma((aggs,)), dma((aggs,)), dma((aggs,)), dma((aggs,)),
            ],
            compiler_params=pltpu.CompilerParams(
                collective_id=0, has_side_effects=True, vmem_limit_bytes=56 * 1024 * 1024
            ),
            cost_estimate=pl.CostEstimate(
                flops=2 * rows * links * blk * blk * nnull, bytes_accessed=rows * links * blk * blk * 2, transcendentals=0
            ),
        )(columns.T, aggregate, coarse_slot.T, send_rows, prolong, blocks)

    return jax.shard_map(
        per_device,
        mesh=mesh,
        in_specs=(
            P(("layer", "tile"), None, None, None),
            P(("layer", "tile"), None),
            P(("layer", "tile"), None),
            P(("layer", "tile")),
            P(("layer", "tile"), None),
            P(("layer", "tile"), None),
        ),
        out_specs=P(("layer", "tile"), None),
        check_vma=False,
    )
```
